256 devices in a mesh: row: 16 (over x_hi, y, core), col: 8 (over z), rep: 2 (over x_lo).
Axes of the slice: x: 4 (x_hi: 2, x_lo: 2; x = x_hi * 2 + x_lo), y: 4, z: 8, core: 2. Of those that a mesh axis runs over, the one named last changes fastest.
Arguments:
- precision: float32 [12288, 12288], P('row', 'col'), may hold values from -1 to 4, as said below
- samples: float32 [1024, 12288], P('rep', 'col'), may hold values from -6 to 6
- new_rows: float32 [512, 12288], P(None, 'row'), may hold values from -6 to 6
- ngram_order: int32 [12288], replicated, may hold values from 1 to 3
Outputs:
- updated: float32 [12288, 12288], P('row', ('col', 'rep'))
- residuals: float32 [512, 12288], P('row', ('col', 'rep'))
The draws below stay inside these ranges and needn't reach their ends.
Inputs may be any that keep to these rules, and one draw needn't show every extreme that they name: `precision`: symmetric; diagonal entries from 1 to 4, off-diagonal entries of magnitude at most 9 / sqrt(12288).
All inputs are finite; a program needn't handle non-finite values.
Results may differ from the reference program's by a relative error of at most 0.0003.
Values sent between devices are 32-bit elements; how exact they have to be, the bound alone decides.
No kernel may reach another device: no remote copies, remote signals or barrier semaphores. Data moves between devices by JAX's collectives and lax.ppermute only.
A program may use at most 128 MiB of HBM per device.

```python
import math
import jax
import jax.numpy as jnp
from jax import lax

P_SIZE = 12288
NEW = 512
SAMPLES = 1024


def draw_precision(key, part):
    first_key, second_key = jax.random.split(key)
    spread = 3.0 / math.sqrt(P_SIZE)
    entries = jax.random.truncated_normal(first_key, -3.0, 3.0, (P_SIZE, P_SIZE), jnp.float32) * spread
    offdiag = (entries + entries.T) * 0.5
    diagonal = jnp.exp(jax.random.uniform(second_key, (P_SIZE,), jnp.float32, 0.0, math.log(4.0)))
    indices = jnp.arange(P_SIZE)
    return jnp.where(indices[:, None] == indices[None, :], diagonal[None, :], offdiag)


def set_ends(values, own_key, smallest, top_value):
    longest = values.shape.index(max(values.shape))
    spots = []
    for shift in (0, 1):
        where = [jax.random.randint(jax.random.fold_in(own_key, axis), (), 0, length) for axis, length in enumerate(values.shape)]
        where[longest] = (where[longest] + shift) % values.shape[longest]
        spots.append(tuple(where))
    return values.at[spots[0]].set(smallest).at[spots[1]].set(top_value)


def block_levels(own_key, shape, pieces, low, largest):
    factor_of = 1.0
    for position, shards_of in pieces:
        draws = jax.random.uniform(jax.random.fold_in(jax.random.fold_in(own_key, 6), position), (shards_of,), jnp.float32, low / len(pieces), largest / len(pieces))
        factor_of = factor_of * jnp.repeat(jnp.exp(draws), shape[position] // shards_of).reshape((-1,) + (1,) * (len(shape) - 1 - position))
    return factor_of


def gaussian(key, dims, scale, reach, cuts=(), dtype=jnp.bfloat16):
    values = scale * jax.random.normal(key, dims, jnp.float32)
    if cuts:
        values = values * block_levels(key, dims, cuts, -0.22, 0.18)
    return jnp.clip(values, -reach, reach).astype(dtype)


def setup_inputs(seed: int = 0) -> dict:
    arg_keys = jax.random.split(jax.random.key(seed), 5)
    return {
        "precision": draw_precision(jax.random.fold_in(arg_keys[4], 71), 0),
        "samples": gaussian(arg_keys[1], (SAMPLES, P_SIZE), 1.0, 6.0, ((0, 2), (1, 8)), jnp.float32),
        "new_rows": gaussian(arg_keys[2], (NEW, P_SIZE), 1.0, 6.0, ((1, 16),), jnp.float32),
        "ngram_order": set_ends(jax.random.randint(arg_keys[3], (P_SIZE,), 1, 4), jax.random.fold_in(arg_keys[3], 1), 1, 3).astype(jnp.int32),
    }


step_size = 0.25
penalty = 0.08


def contract(left, right, left_dim, right_dim):
    return lax.dot_general(left, right, (((left_dim,), (right_dim,)), ((), ())), preferred_element_type=jnp.float32, precision=lax.Precision.HIGHEST)


def reference(precision, samples, new_rows, ngram_order):
    sample_count = samples.shape[0]
    products = contract(precision, samples, 1, 1)
    diagonal = jnp.diagonal(precision)
    orders = ngram_order.astype(jnp.float32)
    block_size = math.gcd(P_SIZE, 1024)
    offsets = (jnp.arange(P_SIZE // block_size) * block_size).astype(jnp.int32)
    columns = jnp.arange(P_SIZE).astype(jnp.int32)

    def update_block(offset):
        prec_rows = lax.dynamic_slice_in_dim(precision, offset, block_size, 0)
        prod_rows = lax.dynamic_slice_in_dim(products, offset, block_size, 0)
        samp_cols = lax.dynamic_slice_in_dim(samples, offset, block_size, 1)
        symmetric = contract(prod_rows, samples, 1, 0) + contract(samp_cols, products, 0, 1)
        row_ids = offset + jnp.arange(block_size).astype(jnp.int32)
        on_diagonal = row_ids[:, None] == columns[None, :]
        inverse_diag = jnp.where(on_diagonal, 1.0 / jnp.where(on_diagonal, prec_rows, 1.0), 0.0)
        gradient = symmetric / (2.0 * sample_count) - inverse_diag
        stepped = prec_rows - step_size * gradient
        row_orders = lax.dynamic_slice_in_dim(orders, offset, block_size, 0)
        threshold = step_size * penalty * 0.5 * (row_orders[:, None] + orders[None, :])
        shrunk = jnp.sign(stepped) * jnp.maximum(jnp.abs(stepped) - threshold, 0.0)
        return jnp.where(on_diagonal, stepped, shrunk)

    updated = lax.map(update_block, offsets).reshape(P_SIZE, P_SIZE)
    residuals = contract(new_rows, updated, 1, 0) / diagonal[None, :]
    return updated, residuals
```

```python
import jax
import jax.numpy as jnp
from jax import lax
from jax.sharding import PartitionSpec as P

step_size = 0.25
penalty = 0.08
AXES = ("row", "col", "rep")
XH, Y, CORE, COL, REP = 2, 4, 2, 8, 2


def contract(left, right, left_dim, right_dim):
    return lax.dot_general(
        left,
        right,
        (((left_dim,), (right_dim,)), ((), ())),
        preferred_element_type=jnp.float32,
        precision=lax.Precision.HIGH,
    )


def send(array, target):
    pairs = []
    for xh in range(XH):
        for y in range(Y):
            for core in range(CORE):
                for z in range(COL):
                    for s in range(REP):
                        place = (xh, y, core, z, s)
                        pairs.append((number(*place), number(*target(*place))))
    return lax.ppermute(array, AXES, pairs)


def number(xh, y, core, z, s):
    return ((((xh * Y + y) * CORE + core) * COL) + z) * REP + s


def to_core(array):
    return send(array, lambda xh, y, core, z, s: (xh, y, 1 - core, z, s))


def to_rep(array):
    return send(array, lambda xh, y, core, z, s: (xh, y, core, z, 1 - s))


def to_xh(array):
    return send(array, lambda xh, y, core, z, s: (1 - xh, y, core, z, s))


def to_z(array, by):
    return send(array, lambda xh, y, core, z, s: (xh, y, core, (z + by) % COL, s))


def to_plane(array, dx, dy):
    return send(array, lambda xh, y, core, z, s: ((xh + dx) % XH, (y + dy) % Y, core, z, s))


def gather_z(piece):
    half = piece.shape[0] // 2
    left, right = [piece], [piece]
    for _ in range(3):
        left.append(to_z(left[-1], 1))
        right.append(to_z(right[-1], -1))
    far = jnp.concatenate([to_z(left[3][:half], 1), to_z(right[3][half:], -1)], 0)
    return [piece, right[1], right[2], right[3], far, left[3], left[2], left[1]]


def scatter_z(whole, z):
    rows = whole.shape[0] // COL
    half = rows // 2

    def own(by):
        return lax.dynamic_slice_in_dim(whole, (z + by) % COL * rows, rows, 0)

    far = own(4)
    up = to_z(far[:half], 1)
    down = to_z(far[half:], -1)
    mine = own(3)
    up = jnp.concatenate([mine[:half] + up, mine[half:]], 0)
    mine = own(5)
    down = jnp.concatenate([mine[:half], mine[half:] + down], 0)
    for by in (2, 1):
        up, down = to_z(up, 1), to_z(down, -1)
        up, down = up + own(by), down + own(COL - by)
    up, down = to_z(up, 1), to_z(down, -1)
    return up + down + own(0)


def rolled(array, by, parts):
    rows = array.shape[0] // parts
    return lax.dynamic_slice_in_dim(jnp.concatenate([array, array], 0), by * rows, array.shape[0], 0)


def per_device(precision, samples, new_rows, ngram_order):
    row_index = lax.axis_index("row")
    z = lax.axis_index("col")
    s = lax.axis_index("rep")
    core = row_index % CORE
    place = row_index // CORE
    xh, y = place // Y, place % Y
    block, tile_cols = precision.shape
    half_samples = samples.shape[0]
    sample_count = half_samples * REP
    slice_rows = half_samples // COL
    own_block = 2 * z + s

    x_own = lax.dynamic_slice_in_dim(samples, s * block, block, 1)
    x_other = to_rep(lax.dynamic_slice_in_dim(samples, (1 - s) * block, block, 1))
    x_piece = lax.dynamic_slice(samples, (place * slice_rows, core * block), (slice_rows, block))
    x_piece = send(x_piece, lambda xh, y, core, z, s: (z // Y, z % Y, core, xh * Y + y, s))
    xi_own = jnp.concatenate(gather_z(x_piece), 0)
    xi_other = to_rep(xi_own)

    prec_half = lax.dynamic_slice_in_dim(precision, s * block, block, 1)
    on_diagonal = (jnp.arange(block)[:, None] == jnp.arange(block)[None, :]) & (row_index == own_block)
    diag = jnp.sum(jnp.where(on_diagonal, prec_half, 0.0), axis=0, keepdims=True)
    diag = diag + to_core(diag)
    diag = diag + to_xh(diag)
    diag = diag + to_plane(diag, 0, 1)
    diag = diag + to_plane(diag, 0, 2)

    piece = scatter_z(contract(samples, precision, 1, 1), z)
    pairs = gather_z(jnp.concatenate([piece, to_rep(piece)], 0))
    prod_rows = jnp.concatenate(pairs, 0)

    turned = send(
        piece,
        lambda xh, y, core, z, s: (z // Y, z % Y, s, xh * Y + y, core),
    )
    two = jnp.concatenate([turned, to_xh(turned)], 0)
    up, down = to_plane(two, 0, 1), to_plane(two, 0, -1)
    far = jnp.concatenate(
        [to_plane(up[:slice_rows], 0, 1), to_plane(down[slice_rows:], 0, -1)], 0
    )
    ring = jnp.stack([two, down, far, up], 0).reshape(Y, XH, slice_rows, block)
    ring = lax.dynamic_slice_in_dim(jnp.concatenate([ring, ring], 0), (Y - y) % Y, Y, 0)
    ring = jnp.where(xh == 0, ring, ring[:, ::-1])
    prod_mine = ring.transpose(1, 0, 2, 3).reshape(half_samples, block)
    prod_swapped = to_core(prod_mine)
    prod_own = rolled(jnp.where(core == s, prod_mine, prod_swapped), z, COL)
    prod_other = rolled(jnp.where(core == s, prod_swapped, prod_mine), z, COL)

    shape = (COL, slice_rows, block)
    x_cols = jnp.stack(
        [rolled(x_own, z, COL).reshape(shape), rolled(x_other, z, COL).reshape(shape)], 1
    ).reshape(sample_count, block)
    symmetric = (
        contract(xi_own, prod_own, 0, 0)
        + contract(xi_other, prod_other, 0, 0)
        + contract(prod_rows, x_cols, 0, 0)
    )
    inverse_diag = jnp.where(on_diagonal, 1.0 / jnp.where(on_diagonal, prec_half, 1.0), 0.0)
    gradient = symmetric / (2.0 * sample_count) - inverse_diag
    stepped = prec_half - step_size * gradient
    orders = ngram_order.astype(jnp.float32)
    order_rows = lax.dynamic_slice_in_dim(orders, row_index * block, block, 0)
    order_cols = lax.dynamic_slice_in_dim(orders, own_block * block, block, 0)
    threshold = step_size * penalty * 0.5 * (order_rows[:, None] + order_cols[None, :])
    shrunk = jnp.sign(stepped) * jnp.maximum(jnp.abs(stepped) - threshold, 0.0)
    updated = jnp.where(on_diagonal, stepped, shrunk)

    partial = contract(new_rows, updated, 1, 0)
    out_rows = partial.shape[0] // (XH * Y * CORE)
    partial = partial.reshape(XH * Y, CORE, out_rows, block)
    kept = lax.dynamic_index_in_dim(partial, core, 1, keepdims=False)
    kept = kept + to_core(lax.dynamic_index_in_dim(partial, 1 - core, 1, keepdims=False))

    def part(dx, dy):
        target = (xh + dx) % XH * Y + (y + dy) % Y
        return lax.dynamic_index_in_dim(kept, target, 0, keepdims=False)

    total = part(0, 0)
    for dx in range(XH):
        for dy in range(Y):
            if dx or dy:
                total = total + to_plane(part(dx, dy), dx, dy)
    return (updated, total / diag)


def solution(mesh):
    placed = (P("row", "col"), P("rep", "col"), P(None, "row"), P())
    return jax.shard_map(
        per_device,
        mesh=mesh,
        in_specs=placed,
        out_specs=(P("row", ("col", "rep")), P("row", ("col", "rep"))),
        check_vma=False,
    )
```

```python
import jax
import jax.numpy as jnp
from jax import lax
from jax.sharding import PartitionSpec as P

step_size = 0.25
penalty = 0.08
AXES = ("row", "col", "rep")
XH, Y, CORE, COL, REP = 2, 4, 2, 8, 2


def contract(left, right, left_dim, right_dim):
    return lax.dot_general(
        left,
        right,
        (((left_dim,), (right_dim,)), ((), ())),
        preferred_element_type=jnp.float32,
        precision=lax.Precision.HIGH,
    )


def send(array, target):
    pairs = []
    for xh in range(XH):
        for y in range(Y):
            for core in range(CORE):
                for z in range(COL):
                    for s in range(REP):
                        place = (xh, y, core, z, s)
                        pairs.append((number(*place), number(*target(*place))))
    return lax.ppermute(array, AXES, pairs)


def number(xh, y, core, z, s):
    return ((((xh * Y + y) * CORE + core) * COL) + z) * REP + s


def to_core(array):
    return send(array, lambda xh, y, core, z, s: (xh, y, 1 - core, z, s))


def to_rep(array):
    return send(array, lambda xh, y, core, z, s: (xh, y, core, z, 1 - s))


def to_xh(array):
    return send(array, lambda xh, y, core, z, s: (1 - xh, y, core, z, s))


def to_z(array, by):
    return send(array, lambda xh, y, core, z, s: (xh, y, core, (z + by) % COL, s))


def to_plane(array, dx, dy):
    return send(array, lambda xh, y, core, z, s: ((xh + dx) % XH, (y + dy) % Y, core, z, s))


def tie(*arrays):
    return lax.optimization_barrier(arrays)


def scatter_z(whole, z):
    rows = whole.shape[0] // COL
    half = rows // 2

    def own(by):
        return lax.dynamic_slice_in_dim(whole, (z + by) % COL * rows, rows, 0)

    far = own(4)
    up = to_z(far[:half], 1)
    down = to_z(far[half:], -1)
    mine = own(3)
    up = jnp.concatenate([mine[:half] + up, mine[half:]], 0)
    mine = own(5)
    down = jnp.concatenate([mine[:half], mine[half:] + down], 0)
    for by in (2, 1):
        up, down = to_z(up, 1), to_z(down, -1)
        up, down = up + own(by), down + own(COL - by)
    up, down = to_z(up, 1), to_z(down, -1)
    return up + down + own(0)


def along_z(array, z):
    turned = lax.dynamic_slice_in_dim(jnp.concatenate([array, array], 0), z, COL, 0)
    order = (0, 7, 1, 6, 2, 5, 3, 4)
    return jnp.concatenate([turned[i] for i in order], 0).reshape(-1, array.shape[-1])


def per_device(precision, samples, new_rows, ngram_order):
    row_index = lax.axis_index("row")
    z = lax.axis_index("col")
    s = lax.axis_index("rep")
    core = row_index % CORE
    place = row_index // CORE
    xh, y = place // Y, place % Y
    block = precision.shape[0]
    half_samples = samples.shape[0]
    sample_count = half_samples * REP
    rows = half_samples // COL
    own_block = 2 * z + s

    x_piece = lax.dynamic_slice(samples, (place * rows, core * block), (rows, block))
    x_piece = send(x_piece, lambda xh, y, core, z, s: (z // Y, z % Y, core, xh * Y + y, s))
    x_own = lax.dynamic_slice_in_dim(samples, s * block, block, 1)
    x_other = to_rep(lax.dynamic_slice_in_dim(samples, (1 - s) * block, block, 1))
    prec_half = lax.dynamic_slice_in_dim(precision, s * block, block, 1)
    on_diagonal = (jnp.arange(block)[:, None] == jnp.arange(block)[None, :]) & (row_index == own_block)
    diag = jnp.sum(jnp.where(on_diagonal, prec_half, 0.0), axis=0, keepdims=True)
    diag = jnp.where(jnp.arange(8)[:, None] == 0, diag, 0.0)

    partial, x_piece = tie(contract(samples, precision, 1, 1), x_piece)
    xr_own = lax.all_gather(x_piece, "col", axis=0, tiled=True)
    piece = scatter_z(partial, z)
    piece, xr_own, x_other, diag = tie(piece, xr_own, x_other, diag)

    swapped, turned = to_rep(piece), send(
        piece,
        lambda xh, y, core, z, s: (z // Y, z % Y, s, xh * Y + y, core),
    )
    swapped, turned, xr_own = tie(swapped, turned, xr_own)
    xr_other = to_rep(xr_own)
    pair = jnp.concatenate([piece, swapped], 0)
    one = jnp.concatenate([turned, diag], 0)
    deep = one.shape[0]
    up1, down1, beside = tie(to_z(pair, 1), to_z(pair, -1), to_xh(one))
    two = jnp.concatenate([one, beside], 0)
    up2, down2, north, south = tie(
        to_z(up1, 1), to_z(down1, -1), to_plane(two, 0, 1), to_plane(two, 0, -1)
    )
    up3, down3, far_north, far_south = tie(
        to_z(up2, 1),
        to_z(down2, -1),
        to_plane(north[:deep], 0, 1),
        to_plane(south[deep:], 0, -1),
    )
    far = [to_z(up3[:rows], 1), to_z(down3[rows:], -1)]
    ring = jnp.stack([two, south, jnp.concatenate([far_north, far_south], 0), north], 0)
    ring = ring.reshape(Y, XH, deep, block)
    ring = lax.dynamic_slice_in_dim(jnp.concatenate([ring, ring], 0), (Y - y) % Y, Y, 0)
    ring = jnp.where(xh == 0, ring, ring[:, ::-1])
    mine = ring.transpose(1, 0, 2, 3).reshape(COL, deep, block)
    others = to_core(mine)
    diag = jnp.sum(mine[:, rows:] + others[:, rows:], axis=(0, 1))[None, :]

    def flat(array):
        return array[:, :rows].reshape(-1, block)

    shape = (COL, rows, block)
    x_cols = along_z(jnp.stack([x_own.reshape(shape), x_other.reshape(shape)], 1), z)
    cut = 5 * 2 * rows
    symmetric = contract(
        jnp.concatenate([pair, up1, down1, up2, down2], 0), x_cols[:cut], 0, 0
    )
    symmetric += contract(jnp.where(core == s, xr_own, xr_other), flat(mine), 0, 0)
    symmetric += contract(jnp.where(core == s, xr_other, xr_own), flat(others), 0, 0)
    symmetric += contract(jnp.concatenate([up3, down3] + far, 0), x_cols[cut:], 0, 0)
    inverse_diag = jnp.where(on_diagonal, 1.0 / jnp.where(on_diagonal, prec_half, 1.0), 0.0)
    gradient = symmetric / (2.0 * sample_count) - inverse_diag
    stepped = prec_half - step_size * gradient
    orders = ngram_order.astype(jnp.float32)
    order_rows = lax.dynamic_slice_in_dim(orders, row_index * block, block, 0)
    order_cols = lax.dynamic_slice_in_dim(orders, own_block * block, block, 0)
    threshold = step_size * penalty * 0.5 * (order_rows[:, None] + order_cols[None, :])
    shrunk = jnp.sign(stepped) * jnp.maximum(jnp.abs(stepped) - threshold, 0.0)
    updated = jnp.where(on_diagonal, stepped, shrunk)

    partial = contract(new_rows, updated, 1, 0)
    out_rows = partial.shape[0] // (XH * Y * CORE)
    partial = partial.reshape(XH * Y, CORE, out_rows, block)
    kept = lax.dynamic_index_in_dim(partial, core, 1, keepdims=False)
    kept = kept + to_core(lax.dynamic_index_in_dim(partial, 1 - core, 1, keepdims=False))

    def part(dx, dy):
        target = (xh + dx) % XH * Y + (y + dy) % Y
        return lax.dynamic_index_in_dim(kept, target, 0, keepdims=False)

    total = part(0, 0)
    for dx in range(XH):
        for dy in range(Y):
            if dx or dy:
                total = total + to_plane(part(dx, dy), dx, dy)
    return (updated, total / diag)


def solution(mesh):
    placed = (P("row", "col"), P("rep", "col"), P(None, "row"), P())
    return jax.shard_map(
        per_device,
        mesh=mesh,
        in_specs=placed,
        out_specs=(P("row", ("col", "rep")), P("row", ("col", "rep"))),
        check_vma=False,
    )
```

```python
import jax
import jax.numpy as jnp
from jax import lax
from jax.sharding import PartitionSpec as P

step_size = 0.25
penalty = 0.08
AXES = ("row", "col", "rep")
XH, Y, CORE, COL, REP = 2, 4, 2, 8, 2
ORDER = (0, 7, 1, 6, 2, 5, 3, 4)


def contract(left, right, left_dim, right_dim):
    return lax.dot_general(
        left,
        right,
        (((left_dim,), (right_dim,)), ((), ())),
        preferred_element_type=jnp.float32,
        precision=lax.Precision.HIGH,
    )


def send(array, target):
    pairs = []
    for xh in range(XH):
        for y in range(Y):
            for core in range(CORE):
                for z in range(COL):
                    for s in range(REP):
                        place = (xh, y, core, z, s)
                        pairs.append((number(*place), number(*target(*place))))
    return lax.ppermute(array, AXES, pairs)


def number(xh, y, core, z, s):
    return ((((xh * Y + y) * CORE + core) * COL) + z) * REP + s


def to_core(array):
    return send(array, lambda xh, y, core, z, s: (xh, y, 1 - core, z, s))


def to_rep(array):
    return send(array, lambda xh, y, core, z, s: (xh, y, core, z, 1 - s))


def to_xh(array):
    return send(array, lambda xh, y, core, z, s: (1 - xh, y, core, z, s))


def to_z(array, by):
    return send(array, lambda xh, y, core, z, s: (xh, y, core, (z + by) % COL, s))


def to_plane(array, dx, dy):
    return send(array, lambda xh, y, core, z, s: ((xh + dx) % XH, (y + dy) % Y, core, z, s))


def tie(*arrays):
    return lax.optimization_barrier(arrays)


def both_z(up, down):
    return tie(to_z(up, 1), to_z(down, -1))


def join(*arrays):
    return jnp.concatenate(arrays, 0)


def scatter_z(whole, x_piece, z):
    rows = whole.shape[0] // COL
    half = rows // 2

    def own(by):
        return lax.dynamic_slice_in_dim(whole, (z + by) % COL * rows, rows, 0)

    far = own(4)
    up, down, x_piece = tie(to_z(far[:half], 1), to_z(far[half:], -1), x_piece)
    after, before = own(3), own(5)
    up = join(after[:half] + up, after[half:])
    down = join(before[:half], before[half:] + down)
    pieces = [x_piece, x_piece, x_piece]
    for by in (2, 1, 0):
        up, down = both_z(join(up, pieces[-2]), join(down, pieces[-1]))
        pieces += [up[rows:], down[rows:]]
        if by:
            up, down = up[:rows] + own(by), down[:rows] + own(COL - by)
    return up[:rows] + down[:rows] + own(0), pieces[2:]


def along_z(array, z):
    turned = lax.dynamic_slice_in_dim(jnp.concatenate([array, array], 0), z, COL, 0)
    return join(*(turned[i % COL] for i in ORDER)).reshape(-1, array.shape[-1])


def per_device(precision, samples, new_rows, ngram_order):
    row_index = lax.axis_index("row")
    z = lax.axis_index("col")
    s = lax.axis_index("rep")
    core = row_index % CORE
    place = row_index // CORE
    xh, y = place // Y, place % Y
    block = precision.shape[0]
    half_samples = samples.shape[0]
    sample_count = half_samples * REP
    rows = half_samples // COL
    own_block = 2 * z + s

    x_piece = lax.dynamic_slice(samples, (place * rows, core * block), (rows, block))
    x_piece = send(x_piece, lambda xh, y, core, z, s: (z // Y, z % Y, core, xh * Y + y, s))
    x_own = lax.dynamic_slice_in_dim(samples, s * block, block, 1)
    x_other = to_rep(lax.dynamic_slice_in_dim(samples, (1 - s) * block, block, 1))
    prec_half = lax.dynamic_slice_in_dim(precision, s * block, block, 1)
    on_diagonal = (jnp.arange(block)[:, None] == jnp.arange(block)[None, :]) & (row_index == own_block)
    diag = jnp.sum(jnp.where(on_diagonal, prec_half, 0.0), axis=0, keepdims=True)
    diag = jnp.where(jnp.arange(8)[:, None] == 0, diag, 0.0)

    piece, x_ring = scatter_z(contract(samples, precision, 1, 1), x_piece, z)
    piece, x_other, diag = tie(piece, x_other, diag)

    half = rows // 2
    turned = send(
        piece,
        lambda xh, y, core, z, s: (z // Y, z % Y, s, xh * Y + y, core),
    )
    swapped, *x_ring = tie(to_rep(piece), *x_ring)
    x_first = to_rep(join(*x_ring[:5]))
    pair = join(piece, swapped)
    up1, down1, turned = tie(
        to_z(join(pair, x_ring[5][:half]), 1), to_z(join(pair, x_ring[6][half:]), -1), turned
    )
    x_ring += [up1[2 * rows :], down1[2 * rows :]]
    up1, down1 = up1[: 2 * rows], down1[: 2 * rows]
    x_last = to_rep(join(*x_ring[5:]))
    one = join(turned, diag)
    deep = one.shape[0]
    up2, down2, beside = tie(to_z(up1, 1), to_z(down1, -1), to_xh(one))
    two = join(one, beside)
    up3, down3, north, south, x_first = tie(
        to_z(up2, 1), to_z(down2, -1), to_plane(two, 0, 1), to_plane(two, 0, -1), x_first
    )
    shape = (COL, rows, block)
    x_cols = along_z(jnp.stack([x_own.reshape(shape), x_other.reshape(shape)], 1), z)
    cut = 5 * 2 * rows
    symmetric = contract(join(pair, up1, down1, up2, down2), x_cols[:cut], 0, 0)
    far_up, far_down, far_north, far_south, x_last, symmetric = tie(
        to_z(up3[:rows], 1),
        to_z(down3[rows:], -1),
        to_plane(north[:deep], 0, 1),
        to_plane(south[deep:], 0, -1),
        x_last,
        symmetric,
    )
    ring = jnp.stack([two, south, join(far_north, far_south), north], 0)
    ring = ring.reshape(Y * XH, deep, block)
    mine = []
    for by in ORDER:
        other_place = (z + by) % COL
        at = (other_place + Y - y) % Y * XH + (other_place // Y + xh) % XH
        mine.append(lax.dynamic_index_in_dim(ring, at, 0, keepdims=False))
    mine = jnp.stack(mine, 0)
    others = to_core(mine)
    diag = jnp.sum(mine[:, rows:] + others[:, rows:], axis=(0, 1))[None, :]

    def flat(array):
        return array[:, :rows].reshape(-1, block)

    xr_own, xr_other = join(*x_ring), join(x_first, x_last)
    symmetric += contract(join(up3, down3, far_up, far_down), x_cols[cut:], 0, 0)
    symmetric += contract(jnp.where(core == s, xr_own, xr_other), flat(mine), 0, 0)
    symmetric += contract(jnp.where(core == s, xr_other, xr_own), flat(others), 0, 0)
    inverse_diag = jnp.where(on_diagonal, 1.0 / jnp.where(on_diagonal, prec_half, 1.0), 0.0)
    gradient = symmetric / (2.0 * sample_count) - inverse_diag
    stepped = prec_half - step_size * gradient
    orders = ngram_order.astype(jnp.float32)
    order_rows = lax.dynamic_slice_in_dim(orders, row_index * block, block, 0)
    order_cols = lax.dynamic_slice_in_dim(orders, own_block * block, block, 0)
    threshold = step_size * penalty * 0.5 * (order_rows[:, None] + order_cols[None, :])
    shrunk = jnp.sign(stepped) * jnp.maximum(jnp.abs(stepped) - threshold, 0.0)
    updated = jnp.where(on_diagonal, stepped, shrunk)

    partial = contract(new_rows, updated, 1, 0)
    out_rows = partial.shape[0] // (XH * Y * CORE)
    partial = partial.reshape(XH * Y, CORE, out_rows, block)
    kept = lax.dynamic_index_in_dim(partial, core, 1, keepdims=False)
    kept = kept + to_core(lax.dynamic_index_in_dim(partial, 1 - core, 1, keepdims=False))

    def part(dx, dy):
        target = (xh + dx) % XH * Y + (y + dy) % Y
        return lax.dynamic_index_in_dim(kept, target, 0, keepdims=False)

    total = part(0, 0)
    for dx in range(XH):
        for dy in range(Y):
            if dx or dy:
                total = total + to_plane(part(dx, dy), dx, dy)
    return (updated, total / diag)


def solution(mesh):
    placed = (P("row", "col"), P("rep", "col"), P(None, "row"), P())
    return jax.shard_map(
        per_device,
        mesh=mesh,
        in_specs=placed,
        out_specs=(P("row", ("col", "rep")), P("row", ("col", "rep"))),
        check_vma=False,
    )
```

```python
import jax
import jax.numpy as jnp
from jax import lax
from jax.sharding import PartitionSpec as P

step_size = 0.25
penalty = 0.08
AXES = ("row", "col", "rep")
XH, Y, CORE, COL, REP = 2, 4, 2, 8, 2
ORDER = (0, 7, 1, 6, 2, 5, 3, 4)


def contract(left, right, left_dim, right_dim):
    return lax.dot_general(
        left,
        right,
        (((left_dim,), (right_dim,)), ((), ())),
        preferred_element_type=jnp.float32,
        precision=lax.Precision.HIGH,
    )


def send(array, target):
    pairs = []
    for xh in range(XH):
        for y in range(Y):
            for core in range(CORE):
                for z in range(COL):
                    for s in range(REP):
                        place = (xh, y, core, z, s)
                        pairs.append((number(*place), number(*target(*place))))
    return lax.ppermute(array, AXES, pairs)


def number(xh, y, core, z, s):
    return ((((xh * Y + y) * CORE + core) * COL) + z) * REP + s


def to_core(array):
    return send(array, lambda xh, y, core, z, s: (xh, y, 1 - core, z, s))


def to_rep(array):
    return send(array, lambda xh, y, core, z, s: (xh, y, core, z, 1 - s))


def to_xh(array):
    return send(array, lambda xh, y, core, z, s: (1 - xh, y, core, z, s))


def to_z(array, by):
    return send(array, lambda xh, y, core, z, s: (xh, y, core, (z + by) % COL, s))


def to_plane(array, dx, dy):
    return send(array, lambda xh, y, core, z, s: ((xh + dx) % XH, (y + dy) % Y, core, z, s))


def tie(*arrays):
    return lax.optimization_barrier(arrays)


def both_z(up, down):
    return tie(to_z(up, 1), to_z(down, -1))


def join(*arrays):
    return jnp.concatenate(arrays, 0)


def along_z(array, z):
    turned = lax.dynamic_slice_in_dim(jnp.concatenate([array, array], 0), z, COL, 0)
    return join(*(turned[i % COL] for i in ORDER)).reshape(-1, array.shape[-1])


def per_device(precision, samples, new_rows, ngram_order):
    row_index = lax.axis_index("row")
    z = lax.axis_index("col")
    s = lax.axis_index("rep")
    core = row_index % CORE
    place = row_index // CORE
    xh, y = place // Y, place % Y
    block = precision.shape[0]
    half_samples = samples.shape[0]
    sample_count = half_samples * REP
    rows = half_samples // COL
    own_block = 2 * z + s

    x_own = lax.dynamic_slice_in_dim(samples, s * block, block, 1)
    x_sent = lax.dynamic_slice_in_dim(samples, (1 - s) * block, block, 1)
    prec_half = lax.dynamic_slice_in_dim(precision, s * block, block, 1)
    on_diagonal = (jnp.arange(block)[:, None] == jnp.arange(block)[None, :]) & (row_index == own_block)
    diag = jnp.sum(jnp.where(on_diagonal, prec_half, 0.0), axis=0, keepdims=True)
    diag = jnp.where(jnp.arange(8)[:, None] == 0, diag, 0.0)

    half = rows // 2
    partial = contract(samples, precision, 1, 1)

    def own(by):
        return lax.dynamic_slice_in_dim(partial, (z + by) % COL * rows, rows, 0)

    x_piece = lax.dynamic_slice(samples, (place * rows, core * block), (rows, block))
    far = own(4)
    up, down, x_piece, x_sent, x_own = tie(
        to_z(far[:half], 1), to_z(far[half:], -1), x_piece, x_sent, x_own
    )
    x_piece = send(x_piece, lambda xh, y, core, z, s: (z // Y, z % Y, core, xh * Y + y, s))
    x_other = to_rep(x_sent)
    after, before = own(3), own(5)
    up, down = both_z(
        join(after[:half] + up, after[half:]), join(before[:half], before[half:] + down)
    )
    up, down, x_piece, diag = tie(to_z(up + own(2), 1), to_z(down + own(6), -1), x_piece, diag)
    up, down = both_z(join(up + own(1), x_piece), join(down + own(7), x_piece))
    x_up1, x_down1 = up[rows:], down[rows:]
    piece = up[:rows] + down[:rows] + own(0)

    swapped, piece, x_up1, x_down1, x_other = tie(to_rep(piece), piece, x_up1, x_down1, x_other)
    pair = join(piece, swapped)
    turned = send(piece, lambda xh, y, core, z, s: (z // Y, z % Y, s, xh * Y + y, core))
    deep = 2 * rows
    up1, down1 = both_z(join(pair, x_up1), join(pair, x_down1))
    x_ring = [x_piece, x_up1, x_down1, up1[deep:], down1[deep:]]
    x_first = to_rep(join(*x_ring))
    up2, down2, turned = tie(to_z(up1, 1), to_z(down1, -1), turned)
    x_ring += [up2[deep:], down2[deep:]]
    up1, down1 = up1[:deep], down1[:deep]
    up3, down3, beside = tie(
        to_z(up2[: deep + half], 1), to_z(join(down2[:deep], down2[deep + half :]), -1), to_xh(join(turned, diag))
    )
    diag += beside[rows:]
    x_ring += [up3[deep:], down3[deep:]]
    up2, down2, up3, down3 = up2[:deep], down2[:deep], up3[:deep], down3[:deep]
    x_last = to_rep(join(*x_ring[5:]))
    two = join(turned, beside[:rows], diag)
    shape = (COL, rows, block)
    x_cols = along_z(jnp.stack([x_own.reshape(shape), x_other.reshape(shape)], 1), z)
    cut = 5 * 2 * rows
    symmetric = contract(join(pair, up1, down1, up2, down2), x_cols[:cut], 0, 0)
    far_up, far_down, north, south, x_first = tie(
        to_z(up3[:rows], 1),
        to_z(down3[rows:], -1),
        to_plane(two, 0, 1),
        to_plane(two, 0, -1),
        x_first,
    )
    far_north, far_south, x_last, symmetric = tie(
        to_plane(join(north[:rows], north[deep:]), 0, 1), to_plane(south[rows:deep], 0, -1), x_last, symmetric
    )
    diag += north[deep:] + south[deep:] + far_north[rows:]
    ring = join(two[:deep], south[:deep], far_north[:rows], far_south, north[:deep])
    ring = ring.reshape(Y * XH, rows, block)
    mine = []
    for by in ORDER:
        other_place = (z + by) % COL
        at = (other_place + Y - y) % Y * XH + (other_place // Y + xh) % XH
        mine.append(lax.dynamic_index_in_dim(ring, at, 0, keepdims=False))
    mine = join(*mine)
    others, diag_other = tie(to_core(mine), to_core(diag))
    diag = (diag + diag_other)[:1]
    xr_own, xr_other = join(*x_ring), join(x_first, x_last)
    symmetric += contract(join(up3, down3, far_up, far_down), x_cols[cut:], 0, 0)
    symmetric += contract(jnp.where(core == s, xr_own, xr_other), mine, 0, 0)
    symmetric += contract(jnp.where(core == s, xr_other, xr_own), others, 0, 0)
    inverse_diag = jnp.where(on_diagonal, 1.0 / jnp.where(on_diagonal, prec_half, 1.0), 0.0)
    gradient = symmetric / (2.0 * sample_count) - inverse_diag
    stepped = prec_half - step_size * gradient
    orders = ngram_order.astype(jnp.float32)
    order_rows = lax.dynamic_slice_in_dim(orders, row_index * block, block, 0)
    order_cols = lax.dynamic_slice_in_dim(orders, own_block * block, block, 0)
    threshold = step_size * penalty * 0.5 * (order_rows[:, None] + order_cols[None, :])
    shrunk = jnp.sign(stepped) * jnp.maximum(jnp.abs(stepped) - threshold, 0.0)
    updated = jnp.where(on_diagonal, stepped, shrunk)

    partial = contract(new_rows, updated, 1, 0)
    out_rows = partial.shape[0] // (XH * Y * CORE)
    partial = partial.reshape(XH * Y, CORE, out_rows, block)
    kept = lax.dynamic_index_in_dim(partial, core, 1, keepdims=False)
    kept = kept + to_core(lax.dynamic_index_in_dim(partial, 1 - core, 1, keepdims=False))

    def part(dx, dy):
        target = (xh + dx) % XH * Y + (y + dy) % Y
        return lax.dynamic_index_in_dim(kept, target, 0, keepdims=False)

    total = part(0, 0)
    for dx in range(XH):
        for dy in range(Y):
            if dx or dy:
                total = total + to_plane(part(dx, dy), dx, dy)
    return (updated, total / diag)


def solution(mesh):
    placed = (P("row", "col"), P("rep", "col"), P(None, "row"), P())
    return jax.shard_map(
        per_device,
        mesh=mesh,
        in_specs=placed,
        out_specs=(P("row", ("col", "rep")), P("row", ("col", "rep"))),
        check_vma=False,
    )
```

```python
import jax
import jax.numpy as jnp
from jax import lax
from jax.sharding import PartitionSpec as P

step_size = 0.25
penalty = 0.08
AXES = ("row", "col", "rep")
XH, Y, CORE, COL, REP = 2, 4, 2, 8, 2
ORDER = (0, 7, 1, 6, 2, 5, 3, 4)


def contract(left, right, left_dim, right_dim):
    return lax.dot_general(
        left,
        right,
        (((left_dim,), (right_dim,)), ((), ())),
        preferred_element_type=jnp.float32,
        precision=lax.Precision.HIGH,
    )


def send(array, target):
    pairs = []
    for xh in range(XH):
        for y in range(Y):
            for core in range(CORE):
                for z in range(COL):
                    for s in range(REP):
                        place = (xh, y, core, z, s)
                        pairs.append((number(*place), number(*target(*place))))
    return lax.ppermute(array, AXES, pairs)


def number(xh, y, core, z, s):
    return ((((xh * Y + y) * CORE + core) * COL) + z) * REP + s


def to_core(array):
    return send(array, lambda xh, y, core, z, s: (xh, y, 1 - core, z, s))


def to_rep(array):
    return send(array, lambda xh, y, core, z, s: (xh, y, core, z, 1 - s))


def to_xh(array):
    return send(array, lambda xh, y, core, z, s: (1 - xh, y, core, z, s))


def to_z(array, by):
    return send(array, lambda xh, y, core, z, s: (xh, y, core, (z + by) % COL, s))


def to_plane(array, dx, dy):
    return send(array, lambda xh, y, core, z, s: ((xh + dx) % XH, (y + dy) % Y, core, z, s))


def apart(number, bits):
    place = number ^ bits
    return place // Y, place % Y


def tie(*arrays):
    return lax.optimization_barrier(arrays)


def both_z(up, down):
    return tie(to_z(up, 1), to_z(down, -1))


def join(*arrays):
    return jnp.concatenate(arrays, 0)


def along_z(array, z):
    turned = lax.dynamic_slice_in_dim(jnp.concatenate([array, array], 0), z, COL, 0)
    return join(*(turned[i % COL] for i in ORDER)).reshape(-1, array.shape[-1])


def per_device(precision, samples, new_rows, ngram_order):
    row_index = lax.axis_index("row")
    z = lax.axis_index("col")
    s = lax.axis_index("rep")
    core = row_index % CORE
    place = row_index // CORE
    xh, y = place // Y, place % Y
    block = precision.shape[0]
    half_samples = samples.shape[0]
    sample_count = half_samples * REP
    rows = half_samples // COL
    own_block = 2 * z + s

    x_own = lax.dynamic_slice_in_dim(samples, s * block, block, 1)
    x_half = half_samples // CORE
    x_sent = lax.dynamic_slice(samples, (core * x_half, (1 - s) * block), (x_half, block))
    prec_half = lax.dynamic_slice_in_dim(precision, s * block, block, 1)
    on_diagonal = (jnp.arange(block)[:, None] == jnp.arange(block)[None, :]) & (row_index == own_block)
    diag = jnp.sum(jnp.where(on_diagonal, prec_half, 0.0), axis=0, keepdims=True)
    diag = jnp.where(jnp.arange(8)[:, None] == 0, diag, 0.0)

    half = rows // 2
    partial = contract(samples, precision, 1, 1)

    def own(by):
        return lax.dynamic_slice_in_dim(partial, (z + by) % COL * rows, rows, 0)

    x_piece = lax.dynamic_slice(samples, ((place ^ z) * rows, core * block), (rows, block))
    far = own(4)
    up, down, x_piece, x_sent, x_own = tie(
        to_z(far[:half], 1), to_z(far[half:], -1), x_piece, x_sent, x_own
    )
    x_piece = send(x_piece, lambda xh, y, core, z, s: (xh, y, core, (xh * Y + y) ^ z, s))
    x_got = to_rep(x_sent)
    after, before = own(3), own(5)
    up, down, x_piece = tie(
        to_z(join(after[:half] + up, after[half:]), 1),
        to_z(join(before[:half], before[half:] + down), -1),
        x_piece,
    )
    x_piece = send(x_piece, lambda xh, y, core, z, s: (*apart(xh * Y + y, z), core, z, s))
    up, down, x_piece, diag, x_got = tie(
        to_z(up + own(2), 1), to_z(down + own(6), -1), x_piece, diag, x_got
    )
    up, down = both_z(join(up + own(1), x_piece), join(down + own(7), x_piece))
    x_up1, x_down1 = up[rows:], down[rows:]
    piece = up[:rows] + down[:rows] + own(0)

    turned = send(piece, lambda xh, y, core, z, s: (*apart(xh * Y + y, z), s, z, core))
    swapped, turned, x_up1, x_down1 = tie(to_rep(piece), turned, x_up1, x_down1)
    pair = join(piece, swapped)
    x_more = to_core(x_got)
    x_other = jnp.where(core == 0, join(x_got, x_more), join(x_more, x_got))
    turned = send(turned, lambda xh, y, core, z, s: (xh, y, core, (xh * Y + y) ^ z, s))
    deep = 2 * rows
    up1, down1, turned = tie(
        to_z(join(pair, x_up1), 1), to_z(join(pair, x_down1), -1), turned
    )
    x_ring = [x_piece, x_up1, x_down1, up1[deep:], down1[deep:]]
    x_first = to_rep(join(*x_ring))
    up2, down2, beside = tie(to_z(up1, 1), to_z(down1, -1), to_xh(join(turned, diag)))
    diag += beside[rows:]
    two = join(turned, beside[:rows], diag)
    x_ring += [up2[deep:], down2[deep:]]
    up1, down1 = up1[:deep], down1[:deep]
    up3, down3, north, south, x_first = tie(
        to_z(up2[: deep + half], 1),
        to_z(join(down2[:deep], down2[deep + half :]), -1),
        to_plane(two, 0, 1),
        to_plane(two, 0, -1),
        x_first,
    )
    x_ring += [up3[deep:], down3[deep:]]
    up2, down2, up3, down3 = up2[:deep], down2[:deep], up3[:deep], down3[:deep]
    x_last = to_rep(join(*x_ring[5:]))
    shape = (COL, rows, block)
    x_cols = along_z(jnp.stack([x_own.reshape(shape), x_other.reshape(shape)], 1), z)
    cut = 5 * 2 * rows
    symmetric = contract(join(pair, up1, down1, up2, down2), x_cols[:cut], 0, 0)
    far_up, far_down, far_north, far_south, x_last, symmetric = tie(
        to_z(up3[:rows], 1),
        to_z(down3[rows:], -1),
        to_plane(join(north[:rows], north[deep:]), 0, 1),
        to_plane(south[rows:deep], 0, -1),
        x_last,
        symmetric,
    )
    diag += north[deep:] + south[deep:] + far_north[rows:]
    ring = join(two[:deep], south[:deep], far_north[:rows], far_south, north[:deep])
    ring = ring.reshape(Y * XH, rows, block)
    mine = []
    for by in ORDER:
        other_place = (z + by) % COL ^ z
        at = (other_place + Y - y) % Y * XH + (other_place // Y + xh) % XH
        mine.append(lax.dynamic_index_in_dim(ring, at, 0, keepdims=False))
    mine = join(*mine)
    others, diag_other = tie(to_core(mine), to_core(diag))
    diag = (diag + diag_other)[:1]
    xr_own, xr_other = join(*x_ring), join(x_first, x_last)
    symmetric += contract(join(up3, down3, far_up, far_down), x_cols[cut:], 0, 0)
    symmetric += contract(jnp.where(core == s, xr_own, xr_other), mine, 0, 0)
    symmetric += contract(jnp.where(core == s, xr_other, xr_own), others, 0, 0)
    inverse_diag = jnp.where(on_diagonal, 1.0 / jnp.where(on_diagonal, prec_half, 1.0), 0.0)
    gradient = symmetric / (2.0 * sample_count) - inverse_diag
    stepped = prec_half - step_size * gradient
    orders = ngram_order.astype(jnp.float32)
    order_rows = lax.dynamic_slice_in_dim(orders, row_index * block, block, 0)
    order_cols = lax.dynamic_slice_in_dim(orders, own_block * block, block, 0)
    threshold = step_size * penalty * 0.5 * (order_rows[:, None] + order_cols[None, :])
    shrunk = jnp.sign(stepped) * jnp.maximum(jnp.abs(stepped) - threshold, 0.0)
    updated = jnp.where(on_diagonal, stepped, shrunk)

    partial = contract(new_rows, updated, 1, 0)
    out_rows = partial.shape[0] // (XH * Y * CORE)
    partial = partial.reshape(XH * Y, CORE, out_rows, block)
    kept = lax.dynamic_index_in_dim(partial, core, 1, keepdims=False)
    kept = kept + to_core(lax.dynamic_index_in_dim(partial, 1 - core, 1, keepdims=False))

    def part(dx, dy):
        target = (xh + dx) % XH * Y + (y + dy) % Y
        return lax.dynamic_index_in_dim(kept, target, 0, keepdims=False)

    total = part(0, 0)
    for dx in range(XH):
        for dy in range(Y):
            if dx or dy:
                total = total + to_plane(part(dx, dy), dx, dy)
    return (updated, total / diag)


def solution(mesh):
    placed = (P("row", "col"), P("rep", "col"), P(None, "row"), P())
    return jax.shard_map(
        per_device,
        mesh=mesh,
        in_specs=placed,
        out_specs=(P("row", ("col", "rep")), P("row", ("col", "rep"))),
        check_vma=False,
    )
```

```python
import jax
import jax.numpy as jnp
from jax import lax
from jax.sharding import PartitionSpec as P

step_size = 0.25
penalty = 0.08
AXES = ("row", "col", "rep")
XH, Y, CORE, COL, REP = 2, 4, 2, 8, 2
ORDER = (0, 7, 1, 6, 2, 5, 3, 4)


def contract(left, right, left_dim, right_dim):
    return lax.dot_general(
        left,
        right,
        (((left_dim,), (right_dim,)), ((), ())),
        preferred_element_type=jnp.float32,
        precision=lax.Precision.HIGH,
    )


def send(array, target):
    pairs = []
    for xh in range(XH):
        for y in range(Y):
            for core in range(CORE):
                for z in range(COL):
                    for s in range(REP):
                        place = (xh, y, core, z, s)
                        pairs.append((number(*place), number(*target(*place))))
    return lax.ppermute(array, AXES, pairs)


def number(xh, y, core, z, s):
    return ((((xh * Y + y) * CORE + core) * COL) + z) * REP + s


def to_core(array):
    return send(array, lambda xh, y, core, z, s: (xh, y, 1 - core, z, s))


def to_rep(array):
    return send(array, lambda xh, y, core, z, s: (xh, y, core, z, 1 - s))


def to_xh(array):
    return send(array, lambda xh, y, core, z, s: (1 - xh, y, core, z, s))


def to_z(array, by):
    return send(array, lambda xh, y, core, z, s: (xh, y, core, (z + by) % COL, s))


def to_plane(array, dx, dy):
    return send(array, lambda xh, y, core, z, s: ((xh + dx) % XH, (y + dy) % Y, core, z, s))


def apart(number, bits):
    place = number ^ bits
    return place // Y, place % Y


def tie(*arrays):
    return lax.optimization_barrier(arrays)


def both_z(up, down):
    return tie(to_z(up, 1), to_z(down, -1))


def join(*arrays):
    return jnp.concatenate(arrays, 0)


def along_z(array, z):
    turned = lax.dynamic_slice_in_dim(jnp.concatenate([array, array], 0), z, COL, 0)
    return join(*(turned[i % COL] for i in ORDER)).reshape(-1, array.shape[-1])


def per_device(precision, samples, new_rows, ngram_order):
    row_index = lax.axis_index("row")
    z = lax.axis_index("col")
    s = lax.axis_index("rep")
    core = row_index % CORE
    place = row_index // CORE
    xh, y = place // Y, place % Y
    block = precision.shape[0]
    half_samples = samples.shape[0]
    sample_count = half_samples * REP
    rows = half_samples // COL
    own_block = 2 * z + s

    x_own = lax.dynamic_slice_in_dim(samples, s * block, block, 1)
    x_half = half_samples // CORE
    x_sent = lax.dynamic_slice(samples, (core * x_half, (1 - s) * block), (x_half, block))
    prec_half = lax.dynamic_slice_in_dim(precision, s * block, block, 1)
    on_diagonal = (jnp.arange(block)[:, None] == jnp.arange(block)[None, :]) & (row_index == own_block)
    diag = jnp.sum(jnp.where(on_diagonal, prec_half, 0.0), axis=0, keepdims=True)
    diag = jnp.where(jnp.arange(8)[:, None] == 0, diag, 0.0)

    x_piece = lax.dynamic_slice(samples, ((place ^ z) * rows, core * block), (rows, block))
    x_piece = send(x_piece, lambda xh, y, core, z, s: (xh, y, core, (xh * Y + y) ^ z, s))

    half = rows // 2
    partial, x_piece = tie(contract(samples, precision, 1, 1), x_piece)
    x_piece = send(x_piece, lambda xh, y, core, z, s: (*apart(xh * Y + y, z), core, z, s))

    def own(by):
        return lax.dynamic_slice_in_dim(partial, (z + by) % COL * rows, rows, 0)

    far = own(4)
    up, down, x_sent = tie(to_z(far[:half], 1), to_z(far[half:], -1), x_sent)
    x_got = to_rep(x_sent)
    after, before = own(3), own(5)
    up, down, x_piece = tie(
        to_z(join(after[:half] + up, after[half:]), 1),
        to_z(join(before[:half], before[half:] + down), -1),
        x_piece,
    )
    up, down, diag, x_got = tie(
        to_z(join(up + own(2), x_piece), 1), to_z(join(down + own(6), x_piece), -1), diag, x_got
    )
    x_ring = [x_piece, up[rows:], down[rows:]]
    up, down = both_z(join(up[:rows] + own(1), x_ring[1]), join(down[:rows] + own(7), x_ring[2]))
    x_ring += [up[rows:], down[rows:]]
    piece = up[:rows] + down[:rows] + own(0)

    turned = send(piece, lambda xh, y, core, z, s: (*apart(xh * Y + y, z), s, z, core))
    swapped, turned, x_own, *x_ring = tie(to_rep(piece), turned, x_own, *x_ring)
    x_first = to_rep(join(*x_ring))
    x_more = to_core(x_got)
    x_other = jnp.where(core == 0, join(x_got, x_more), join(x_more, x_got))
    turned = send(turned, lambda xh, y, core, z, s: (xh, y, core, (xh * Y + y) ^ z, s))
    pair = join(piece, swapped)
    deep = 2 * rows
    up1, down1, turned = tie(
        to_z(join(pair, x_ring[3]), 1), to_z(join(pair, x_ring[4]), -1), turned
    )
    x_ring += [up1[deep:], down1[deep:]]
    up2, down2, beside = tie(
        to_z(up1[: deep + half], 1),
        to_z(join(down1[:deep], down1[deep + half :]), -1),
        to_xh(join(turned, diag)),
    )
    x_ring += [up2[deep:], down2[deep:]]
    x_last = to_rep(join(*x_ring[5:]))
    up1, down1, up2, down2 = up1[:deep], down1[:deep], up2[:deep], down2[:deep]
    diag += beside[rows:]
    two = join(turned, beside[:rows], diag)
    up3, down3, north, south, x_first = tie(
        to_z(up2, 1), to_z(down2, -1), to_plane(two, 0, 1), to_plane(two, 0, -1), x_first
    )
    shape = (COL, rows, block)
    x_cols = along_z(jnp.stack([x_own.reshape(shape), x_other.reshape(shape)], 1), z)
    cut = 5 * 2 * rows
    symmetric = contract(join(pair, up1, down1, up2, down2), x_cols[:cut], 0, 0)
    far_up, far_down, far_north, far_south, x_last = tie(
        to_z(up3[:rows], 1),
        to_z(down3[rows:], -1),
        to_plane(join(north[:rows], north[deep:]), 0, 1),
        to_plane(south[rows:deep], 0, -1),
        x_last,
    )
    diag += north[deep:] + south[deep:] + far_north[rows:]
    ring = join(two[:deep], south[:deep], far_north[:rows], far_south, north[:deep])
    ring = ring.reshape(Y * XH, rows, block)
    mine = []
    for by in ORDER:
        other_place = (z + by) % COL ^ z
        at = (other_place + Y - y) % Y * XH + (other_place // Y + xh) % XH
        mine.append(lax.dynamic_index_in_dim(ring, at, 0, keepdims=False))
    mine = join(*mine)
    others, diag_other, symmetric = tie(to_core(mine), to_core(diag), symmetric)
    diag = (diag + diag_other)[:1]
    xr_own, xr_other = join(*x_ring), join(x_first, x_last)
    symmetric += contract(join(up3, down3, far_up, far_down), x_cols[cut:], 0, 0)
    symmetric += contract(jnp.where(core == s, xr_own, xr_other), mine, 0, 0)
    symmetric += contract(jnp.where(core == s, xr_other, xr_own), others, 0, 0)
    inverse_diag = jnp.where(on_diagonal, 1.0 / jnp.where(on_diagonal, prec_half, 1.0), 0.0)
    gradient = symmetric / (2.0 * sample_count) - inverse_diag
    stepped = prec_half - step_size * gradient
    orders = ngram_order.astype(jnp.float32)
    order_rows = lax.dynamic_slice_in_dim(orders, row_index * block, block, 0)
    order_cols = lax.dynamic_slice_in_dim(orders, own_block * block, block, 0)
    threshold = step_size * penalty * 0.5 * (order_rows[:, None] + order_cols[None, :])
    shrunk = jnp.sign(stepped) * jnp.maximum(jnp.abs(stepped) - threshold, 0.0)
    updated = jnp.where(on_diagonal, stepped, shrunk)

    partial = contract(new_rows, updated, 1, 0)
    out_rows = partial.shape[0] // (XH * Y * CORE)
    partial = partial.reshape(XH * Y, CORE, out_rows, block)
    kept = lax.dynamic_index_in_dim(partial, core, 1, keepdims=False)
    kept = kept + to_core(lax.dynamic_index_in_dim(partial, 1 - core, 1, keepdims=False))

    def part(dx, dy):
        target = (xh + dx) % XH * Y + (y + dy) % Y
        return lax.dynamic_index_in_dim(kept, target, 0, keepdims=False)

    total = part(0, 0)
    for dx in range(XH):
        for dy in range(Y):
            if dx or dy:
                total = total + to_plane(part(dx, dy), dx, dy)
    return (updated, total / diag)


def solution(mesh):
    placed = (P("row", "col"), P("rep", "col"), P(None, "row"), P())
    return jax.shard_map(
        per_device,
        mesh=mesh,
        in_specs=placed,
        out_specs=(P("row", ("col", "rep")), P("row", ("col", "rep"))),
        check_vma=False,
    )
```

```python
import jax
import jax.numpy as jnp
from jax import lax
from jax.sharding import PartitionSpec as P

step_size = 0.25
penalty = 0.08
AXES = ("row", "col", "rep")
XH, Y, CORE, COL, REP = 2, 4, 2, 8, 2
ORDER = (0, 7, 1, 6, 2, 5, 3, 4)


def contract(left, right, left_dim, right_dim):
    return lax.dot_general(
        left,
        right,
        (((left_dim,), (right_dim,)), ((), ())),
        preferred_element_type=jnp.float32,
        precision=lax.Precision.HIGH,
    )


def send(array, target):
    pairs = []
    for xh in range(XH):
        for y in range(Y):
            for core in range(CORE):
                for z in range(COL):
                    for s in range(REP):
                        place = (xh, y, core, z, s)
                        pairs.append((number(*place), number(*target(*place))))
    return lax.ppermute(array, AXES, pairs)


def number(xh, y, core, z, s):
    return ((((xh * Y + y) * CORE + core) * COL) + z) * REP + s


def to_core(array):
    return send(array, lambda xh, y, core, z, s: (xh, y, 1 - core, z, s))


def to_rep(array):
    return send(array, lambda xh, y, core, z, s: (xh, y, core, z, 1 - s))


def to_xh(array):
    return send(array, lambda xh, y, core, z, s: (1 - xh, y, core, z, s))


def to_z(array, by):
    return send(array, lambda xh, y, core, z, s: (xh, y, core, (z + by) % COL, s))


def to_plane(array, dx, dy):
    return send(array, lambda xh, y, core, z, s: ((xh + dx) % XH, (y + dy) % Y, core, z, s))


def plane(place):
    return place % COL // Y, place % Y


def tie(*arrays):
    return lax.optimization_barrier(arrays)


def both_z(up, down):
    return tie(to_z(up, 1), to_z(down, -1))


def join(*arrays):
    return jnp.concatenate(arrays, 0)


def along_z(array, z):
    turned = lax.dynamic_slice_in_dim(jnp.concatenate([array, array], 0), z, COL, 0)
    return join(*(turned[i % COL] for i in ORDER)).reshape(-1, array.shape[-1])


def per_device(precision, samples, new_rows, ngram_order):
    row_index = lax.axis_index("row")
    z = lax.axis_index("col")
    s = lax.axis_index("rep")
    core = row_index % CORE
    place = row_index // CORE
    xh, y = place // Y, place % Y
    block = precision.shape[0]
    half_samples = samples.shape[0]
    sample_count = half_samples * REP
    rows = half_samples // COL
    own_block = 2 * z + s

    x_own = lax.dynamic_slice_in_dim(samples, s * block, block, 1)
    x_half = half_samples // CORE
    x_sent = lax.dynamic_slice(samples, (core * x_half, (1 - s) * block), (x_half, block))
    prec_half = lax.dynamic_slice_in_dim(precision, s * block, block, 1)
    on_diagonal = (jnp.arange(block)[:, None] == jnp.arange(block)[None, :]) & (row_index == own_block)
    diag = jnp.sum(jnp.where(on_diagonal, prec_half, 0.0), axis=0, keepdims=True)
    diag = jnp.where(jnp.arange(8)[:, None] == 0, diag, 0.0)

    x_piece = lax.dynamic_slice(samples, ((place - z) % COL * rows, core * block), (rows, block))
    x_piece = send(x_piece, lambda xh, y, core, z, s: (xh, y, core, (xh * Y + y - z) % COL, s))

    half = rows // 2
    partial, x_piece, x_sent, diag = tie(contract(samples, precision, 1, 1), x_piece, x_sent, diag)
    x_piece = send(x_piece, lambda xh, y, core, z, s: (*plane(xh * Y + y - z), core, z, s))

    def own(by):
        return lax.dynamic_slice_in_dim(partial, (z + by) % COL * rows, rows, 0)

    far = own(4)
    up, down = both_z(far[:half], far[half:])
    x_got = to_rep(x_sent)
    after, before = own(3), own(5)
    up, down, x_piece = tie(
        to_z(join(after[:half] + up, after[half:]), 1),
        to_z(join(before[:half], before[half:] + down), -1),
        x_piece,
    )
    up, down, x_got = tie(
        to_z(join(up + own(2), x_piece), 1), to_z(join(down + own(6), x_piece), -1), x_got
    )
    x_ring = [x_piece, up[rows:], down[rows:]]
    up, down = both_z(join(up[:rows] + own(1), x_ring[1]), join(down[:rows] + own(7), x_ring[2]))
    x_ring += [up[rows:], down[rows:]]
    piece = up[:rows] + down[:rows] + own(0)

    turned = send(piece, lambda xh, y, core, z, s: (*plane(xh * Y + y + z), s, z, core))
    swapped, turned, x_own, *x_ring = tie(to_rep(piece), turned, x_own, *x_ring)
    x_first = to_rep(join(*x_ring))
    x_more = to_core(x_got)
    x_other = jnp.where(core == 0, join(x_got, x_more), join(x_more, x_got))
    turned = send(turned, lambda xh, y, core, z, s: (xh, y, core, (xh * Y + y - z) % COL, s))
    pair = join(piece, swapped)
    deep = 2 * rows
    up1, down1, turned = tie(
        to_z(join(pair, x_ring[3]), 1), to_z(join(pair, x_ring[4]), -1), turned
    )
    x_ring += [up1[deep:], down1[deep:]]
    up2, down2, beside = tie(
        to_z(up1[: deep + half], 1),
        to_z(join(down1[:deep], down1[deep + half :]), -1),
        to_xh(join(turned, diag)),
    )
    x_ring += [up2[deep:], down2[deep:]]
    x_last = to_rep(join(*x_ring[5:]))
    up1, down1, up2, down2 = up1[:deep], down1[:deep], up2[:deep], down2[:deep]
    diag += beside[rows:]
    two = join(turned, beside[:rows], diag)
    up3, down3, north, south, x_first = tie(
        to_z(up2, 1), to_z(down2, -1), to_plane(two, 0, 1), to_plane(two, 0, -1), x_first
    )
    shape = (COL, rows, block)
    x_cols = along_z(jnp.stack([x_own.reshape(shape), x_other.reshape(shape)], 1), z)
    cut = 5 * 2 * rows
    symmetric = contract(join(pair, up1, down1, up2, down2), x_cols[:cut], 0, 0)
    far_up, far_down, far_north, far_south, x_last = tie(
        to_z(up3[:rows], 1),
        to_z(down3[rows:], -1),
        to_plane(join(north[:rows], north[deep:]), 0, 1),
        to_plane(south[rows:deep], 0, -1),
        x_last,
    )
    diag += north[deep:] + south[deep:] + far_north[rows:]
    ring = join(two[:deep], south[:deep], far_north[:rows], far_south, north[:deep])
    ring = ring.reshape(Y * XH, rows, block)
    mine = []
    for by in ORDER:
        other_place = (z + by + z) % COL
        at = (other_place + Y - y) % Y * XH + (other_place // Y + xh) % XH
        mine.append(lax.dynamic_index_in_dim(ring, at, 0, keepdims=False))
    mine = join(*mine)
    others, diag_other, symmetric = tie(to_core(mine), to_core(diag), symmetric)
    diag = (diag + diag_other)[:1]
    xr_own, xr_other = join(*x_ring), join(x_first, x_last)
    symmetric += contract(join(up3, down3, far_up, far_down), x_cols[cut:], 0, 0)
    symmetric += contract(jnp.where(core == s, xr_own, xr_other), mine, 0, 0)
    symmetric += contract(jnp.where(core == s, xr_other, xr_own), others, 0, 0)
    inverse_diag = jnp.where(on_diagonal, 1.0 / jnp.where(on_diagonal, prec_half, 1.0), 0.0)
    gradient = symmetric / (2.0 * sample_count) - inverse_diag
    stepped = prec_half - step_size * gradient
    orders = ngram_order.astype(jnp.float32)
    order_rows = lax.dynamic_slice_in_dim(orders, row_index * block, block, 0)
    order_cols = lax.dynamic_slice_in_dim(orders, own_block * block, block, 0)
    threshold = step_size * penalty * 0.5 * (order_rows[:, None] + order_cols[None, :])
    shrunk = jnp.sign(stepped) * jnp.maximum(jnp.abs(stepped) - threshold, 0.0)
    updated = jnp.where(on_diagonal, stepped, shrunk)

    partial = contract(new_rows, updated, 1, 0)
    out_rows = partial.shape[0] // (XH * Y * CORE)
    partial = partial.reshape(XH * Y, CORE, out_rows, block)
    kept = lax.dynamic_index_in_dim(partial, core, 1, keepdims=False)
    kept = kept + to_core(lax.dynamic_index_in_dim(partial, 1 - core, 1, keepdims=False))

    def part(dx, dy):
        target = (xh + dx) % XH * Y + (y + dy) % Y
        return lax.dynamic_index_in_dim(kept, target, 0, keepdims=False)

    total = part(0, 0)
    for dx in range(XH):
        for dy in range(Y):
            if dx or dy:
                total = total + to_plane(part(dx, dy), dx, dy)
    return (updated, total / diag)


def solution(mesh):
    placed = (P("row", "col"), P("rep", "col"), P(None, "row"), P())
    return jax.shard_map(
        per_device,
        mesh=mesh,
        in_specs=placed,
        out_specs=(P("row", ("col", "rep")), P("row", ("col", "rep"))),
        check_vma=False,
    )
```

```python
import jax
import jax.numpy as jnp
from jax import lax
from jax.sharding import PartitionSpec as P

step_size = 0.25
penalty = 0.08
AXES = ("row", "col", "rep")
XH, Y, CORE, COL, REP = 2, 4, 2, 8, 2
ORDER = (0, 7, 1, 6, 2, 5, 3, 4)


def contract(left, right, left_dim, right_dim):
    return lax.dot_general(
        left,
        right,
        (((left_dim,), (right_dim,)), ((), ())),
        preferred_element_type=jnp.float32,
        precision=lax.Precision.HIGH,
    )


def send(array, target):
    pairs = []
    for xh in range(XH):
        for y in range(Y):
            for core in range(CORE):
                for z in range(COL):
                    for s in range(REP):
                        place = (xh, y, core, z, s)
                        pairs.append((number(*place), number(*target(*place))))
    return lax.ppermute(array, AXES, pairs)


def number(xh, y, core, z, s):
    return ((((xh * Y + y) * CORE + core) * COL) + z) * REP + s


def to_core(array):
    return send(array, lambda xh, y, core, z, s: (xh, y, 1 - core, z, s))


def to_rep(array):
    return send(array, lambda xh, y, core, z, s: (xh, y, core, z, 1 - s))


def to_xh(array):
    return send(array, lambda xh, y, core, z, s: (1 - xh, y, core, z, s))


def to_z(array, by):
    return send(array, lambda xh, y, core, z, s: (xh, y, core, (z + by) % COL, s))


def to_plane(array, dx, dy):
    return send(array, lambda xh, y, core, z, s: ((xh + dx) % XH, (y + dy) % Y, core, z, s))


def plane(place):
    return place % COL // Y, place % Y


def tie(*arrays):
    return lax.optimization_barrier(arrays)


def both_z(up, down):
    return tie(to_z(up, 1), to_z(down, -1))


def join(*arrays):
    return jnp.concatenate(arrays, 0)


def along_z(array, z):
    array = array.reshape(COL, -1, array.shape[-1])
    turned = lax.dynamic_slice_in_dim(join(array, array), z, COL, 0)
    return join(*(turned[i] for i in ORDER))


def per_device(precision, samples, new_rows, ngram_order):
    row_index = lax.axis_index("row")
    z = lax.axis_index("col")
    s = lax.axis_index("rep")
    core = row_index % CORE
    place = row_index // CORE
    xh, y = place // Y, place % Y
    block = precision.shape[0]
    half_samples = samples.shape[0]
    sample_count = half_samples * REP
    rows = half_samples // COL
    own_block = 2 * z + s

    x_own = lax.dynamic_slice_in_dim(samples, s * block, block, 1)
    x_half = half_samples // CORE
    x_sent = lax.dynamic_slice(samples, (core * x_half, (1 - s) * block), (x_half, block))
    prec_half = lax.dynamic_slice_in_dim(precision, s * block, block, 1)
    on_diagonal = (jnp.arange(block)[:, None] == jnp.arange(block)[None, :]) & (row_index == own_block)
    diag = jnp.sum(jnp.where(on_diagonal, prec_half, 0.0), axis=0, keepdims=True)
    diag = jnp.where(jnp.arange(8)[:, None] == 0, diag, 0.0)

    x_piece = lax.dynamic_slice(samples, ((place - z) % COL * rows, core * block), (rows, block))
    x_piece = send(x_piece, lambda xh, y, core, z, s: (xh, y, core, (xh * Y + y - z) % COL, s))

    half = rows // 2
    partial, x_piece, x_sent, diag = tie(contract(samples, precision, 1, 1), x_piece, x_sent, diag)
    x_piece = send(x_piece, lambda xh, y, core, z, s: (*plane(xh * Y + y - z), core, z, s))

    def own(by):
        return lax.dynamic_slice_in_dim(partial, (z + by) % COL * rows, rows, 0)

    far = own(4)
    up, down = both_z(far[:half], far[half:])
    x_got = to_rep(x_sent)
    after, before = own(3), own(5)
    up, down, x_piece = tie(
        to_z(join(after[:half] + up, after[half:]), 1),
        to_z(join(before[:half], before[half:] + down), -1),
        x_piece,
    )
    up, down, x_got = tie(
        to_z(join(up + own(2), x_piece), 1), to_z(join(down + own(6), x_piece), -1), x_got
    )
    x_ring = [x_piece, up[rows:], down[rows:]]
    up, down = both_z(join(up[:rows] + own(1), x_ring[1]), join(down[:rows] + own(7), x_ring[2]))
    x_ring += [up[rows:], down[rows:]]
    piece = up[:rows] + down[:rows] + own(0)

    turned = send(piece, lambda xh, y, core, z, s: (*plane(xh * Y + y + z), s, z, core))
    up, down, swapped, turned, x_own, *x_ring = tie(
        to_z(join(piece, x_ring[3]), 1),
        to_z(join(piece, x_ring[4]), -1),
        to_rep(piece),
        turned,
        x_own,
        *x_ring,
    )
    own_rows, other_rows = [piece, up[:rows], down[:rows]], [swapped]
    x_first = to_rep(join(*x_ring))
    x_ring += [up[rows:], down[rows:]]
    x_more = to_core(x_got)
    turned = send(turned, lambda xh, y, core, z, s: (xh, y, core, (xh * Y + y - z) % COL, s))
    deep = 2 * rows
    up, down, turned, x_own, x_more = tie(
        to_z(join(up[:rows], swapped, up[rows : rows + half]), 1),
        to_z(join(down[:rows], swapped, down[rows + half :]), -1),
        turned,
        x_own,
        x_more,
    )
    x_other = jnp.where(core == 0, join(x_got, x_more), join(x_more, x_got))
    own_rows += [up[:rows], down[:rows]]
    other_rows += [up[rows:deep], down[rows:deep]]
    x_ring += [up[deep:], down[deep:]]
    up, down, beside, x_last = tie(
        to_z(up[:deep], 1), to_z(down[:deep], -1), to_xh(join(turned, diag)), join(*x_ring[5:])
    )
    own_rows += [up[:rows], down[:rows]]
    other_rows += [up[rows:], down[rows:]]
    x_last = to_rep(x_last)
    diag += beside[rows:]
    two = join(turned, beside[:rows], diag)
    x_own, x_other = along_z(x_own, z), along_z(x_other, z)
    own_cut, other_cut = 7 * rows, 5 * rows
    symmetric = contract(
        join(*own_rows, *other_rows), join(x_own[:own_cut], x_other[:other_cut]), 0, 0
    )
    up, down, north, south, x_first, symmetric = tie(
        to_z(join(up[:half], up[rows:]), 1),
        to_z(join(down[half:rows], down[rows:]), -1),
        to_plane(two, 0, 1),
        to_plane(two, 0, -1),
        x_first,
        symmetric,
    )
    last_rows = [up[:half], down[:half], up[half:], down[half:]]
    up, down, far_north, far_south, x_last = tie(
        to_z(up[half:rows], 1),
        to_z(down[rows:], -1),
        to_plane(join(north[:rows], north[deep:]), 0, 1),
        to_plane(south[rows:deep], 0, -1),
        x_last,
    )
    last_rows += [up, down]
    diag += north[deep:] + south[deep:] + far_north[rows:]
    ring = join(two[:deep], south[:deep], far_north[:rows], far_south, north[:deep])
    ring = ring.reshape(Y * XH, rows, block)
    mine = []
    for by in ORDER:
        other_place = (z + by + z) % COL
        at = (other_place + Y - y) % Y * XH + (other_place // Y + xh) % XH
        mine.append(lax.dynamic_index_in_dim(ring, at, 0, keepdims=False))
    mine = join(*mine)
    others, diag_other = tie(to_core(mine), to_core(diag))
    diag = (diag + diag_other)[:1]
    xr_own, xr_other = join(*x_ring), join(x_first, x_last)
    symmetric += contract(
        join(*last_rows), join(x_own[own_cut:], x_other[other_cut:]), 0, 0
    )
    symmetric += contract(jnp.where(core == s, xr_own, xr_other), mine, 0, 0)
    symmetric += contract(jnp.where(core == s, xr_other, xr_own), others, 0, 0)
    inverse_diag = jnp.where(on_diagonal, 1.0 / jnp.where(on_diagonal, prec_half, 1.0), 0.0)
    gradient = symmetric / (2.0 * sample_count) - inverse_diag
    stepped = prec_half - step_size * gradient
    orders = ngram_order.astype(jnp.float32)
    order_rows = lax.dynamic_slice_in_dim(orders, row_index * block, block, 0)
    order_cols = lax.dynamic_slice_in_dim(orders, own_block * block, block, 0)
    threshold = step_size * penalty * 0.5 * (order_rows[:, None] + order_cols[None, :])
    shrunk = jnp.sign(stepped) * jnp.maximum(jnp.abs(stepped) - threshold, 0.0)
    updated = jnp.where(on_diagonal, stepped, shrunk)

    partial = contract(new_rows, updated, 1, 0)
    out_rows = partial.shape[0] // (XH * Y * CORE)
    partial = partial.reshape(XH * Y, CORE, out_rows, block)
    kept = lax.dynamic_index_in_dim(partial, core, 1, keepdims=False)
    kept = kept + to_core(lax.dynamic_index_in_dim(partial, 1 - core, 1, keepdims=False))

    def part(dx, dy):
        target = (xh + dx) % XH * Y + (y + dy) % Y
        return lax.dynamic_index_in_dim(kept, target, 0, keepdims=False)

    total = part(0, 0)
    for dx in range(XH):
        for dy in range(Y):
            if dx or dy:
                total = total + to_plane(part(dx, dy), dx, dy)
    return (updated, total / diag)


def solution(mesh):
    placed = (P("row", "col"), P("rep", "col"), P(None, "row"), P())
    return jax.shard_map(
        per_device,
        mesh=mesh,
        in_specs=placed,
        out_specs=(P("row", ("col", "rep")), P("row", ("col", "rep"))),
        check_vma=False,
    )
```

```python
import jax
import jax.numpy as jnp
from jax import lax
from jax.sharding import PartitionSpec as P

step_size = 0.25
penalty = 0.08
AXES = ("row", "col", "rep")
XH, Y, CORE, COL, REP = 2, 4, 2, 8, 2
ORDER = (0, 7, 1, 6, 2, 5, 3, 4)


def contract(left, right, left_dim, right_dim):
    return lax.dot_general(
        left,
        right,
        (((left_dim,), (right_dim,)), ((), ())),
        preferred_element_type=jnp.float32,
        precision=lax.Precision.HIGH,
    )


def send(array, target):
    pairs = []
    for xh in range(XH):
        for y in range(Y):
            for core in range(CORE):
                for z in range(COL):
                    for s in range(REP):
                        place = (xh, y, core, z, s)
                        pairs.append((number(*place), number(*target(*place))))
    return lax.ppermute(array, AXES, pairs)


def number(xh, y, core, z, s):
    return ((((xh * Y + y) * CORE + core) * COL) + z) * REP + s


def to_core(array):
    return send(array, lambda xh, y, core, z, s: (xh, y, 1 - core, z, s))


def to_rep(array):
    return send(array, lambda xh, y, core, z, s: (xh, y, core, z, 1 - s))


def to_xh(array):
    return send(array, lambda xh, y, core, z, s: (1 - xh, y, core, z, s))


def to_z(array, by):
    return send(array, lambda xh, y, core, z, s: (xh, y, core, (z + by) % COL, s))


def to_plane(array, dx, dy):
    return send(array, lambda xh, y, core, z, s: ((xh + dx) % XH, (y + dy) % Y, core, z, s))


def plane(place):
    return place % COL // Y, place % Y


def tie(*arrays):
    return lax.optimization_barrier(arrays)


def both_z(up, down):
    return tie(to_z(up, 1), to_z(down, -1))


def join(*arrays):
    return jnp.concatenate(arrays, 0)


def along_z(array, z):
    turned = lax.dynamic_slice_in_dim(jnp.concatenate([array, array], 0), z, COL, 0)
    return join(*(turned[i % COL] for i in ORDER)).reshape(-1, array.shape[-1])


def per_device(precision, samples, new_rows, ngram_order):
    row_index = lax.axis_index("row")
    z = lax.axis_index("col")
    s = lax.axis_index("rep")
    core = row_index % CORE
    place = row_index // CORE
    xh, y = place // Y, place % Y
    block = precision.shape[0]
    half_samples = samples.shape[0]
    sample_count = half_samples * REP
    rows = half_samples // COL
    own_block = 2 * z + s

    x_own = lax.dynamic_slice_in_dim(samples, s * block, block, 1)
    x_half = half_samples // CORE
    x_sent = lax.dynamic_slice(samples, (core * x_half, (1 - s) * block), (x_half, block))
    prec_half = lax.dynamic_slice_in_dim(precision, s * block, block, 1)
    on_diagonal = (jnp.arange(block)[:, None] == jnp.arange(block)[None, :]) & (row_index == own_block)
    diag = jnp.sum(jnp.where(on_diagonal, prec_half, 0.0), axis=0, keepdims=True)
    diag = jnp.where(jnp.arange(8)[:, None] == 0, diag, 0.0)

    x_piece = lax.dynamic_slice(samples, ((place - z) % COL * rows, core * block), (rows, block))
    x_piece = send(x_piece, lambda xh, y, core, z, s: (xh, y, core, (xh * Y + y - z) % COL, s))

    half = rows // 2
    partial, x_piece, x_sent, diag = tie(contract(samples, precision, 1, 1), x_piece, x_sent, diag)
    x_piece = send(x_piece, lambda xh, y, core, z, s: (*plane(xh * Y + y - z), core, z, s))

    def own(by):
        return lax.dynamic_slice_in_dim(partial, (z + by) % COL * rows, rows, 0)

    far = own(4)
    up, down = both_z(far[:half], far[half:])
    x_got = to_rep(x_sent)
    after, before = own(3), own(5)
    up, down, x_piece = tie(
        to_z(join(after[:half] + up, after[half:]), 1),
        to_z(join(before[:half], before[half:] + down), -1),
        x_piece,
    )
    up, down, x_got = tie(
        to_z(join(up + own(2), x_piece), 1), to_z(join(down + own(6), x_piece), -1), x_got
    )
    x_ring = [x_piece, up[rows:], down[rows:]]
    up, down = both_z(join(up[:rows] + own(1), x_ring[1]), join(down[:rows] + own(7), x_ring[2]))
    x_ring += [up[rows:], down[rows:]]
    piece = up[:rows] + down[:rows] + own(0)

    turned = send(piece, lambda xh, y, core, z, s: (*plane(xh * Y + y + z), s, z, core))
    swapped, turned, x_own, *x_ring = tie(to_rep(piece), turned, x_own, *x_ring)
    x_first = to_rep(join(*x_ring))
    x_more = to_core(x_got)
    x_other = jnp.where(core == 0, join(x_got, x_more), join(x_more, x_got))
    turned = send(turned, lambda xh, y, core, z, s: (xh, y, core, (xh * Y + y - z) % COL, s))
    pair = join(piece, swapped)
    deep = 2 * rows
    up1, down1, turned = tie(
        to_z(join(pair, x_ring[3]), 1), to_z(join(pair, x_ring[4]), -1), turned
    )
    x_ring += [up1[deep:], down1[deep:]]
    up2, down2, beside = tie(
        to_z(up1[: deep + half], 1),
        to_z(join(down1[:deep], down1[deep + half :]), -1),
        to_xh(join(turned, diag)),
    )
    x_ring += [up2[deep:], down2[deep:]]
    x_last = to_rep(join(*x_ring[5:]))
    up1, down1, up2, down2 = up1[:deep], down1[:deep], up2[:deep], down2[:deep]
    diag += beside[rows:]
    two = join(turned, beside[:rows], diag)
    shape = (COL, rows, block)
    x_cols = along_z(jnp.stack([x_own.reshape(shape), x_other.reshape(shape)], 1), z)
    cut = 5 * 2 * rows
    symmetric = contract(join(pair, up1, down1, up2, down2), x_cols[:cut], 0, 0)
    up3, down3, north, south, x_first, symmetric = tie(
        to_z(up2, 1),
        to_z(down2, -1),
        to_plane(two, 0, 1),
        to_plane(two, 0, -1),
        x_first,
        symmetric,
    )
    far_up, far_down, far_north, far_south, x_last = tie(
        to_z(up3[:rows], 1),
        to_z(down3[rows:], -1),
        to_plane(join(north[:rows], north[deep:]), 0, 1),
        to_plane(south[rows:deep], 0, -1),
        x_last,
    )
    diag += north[deep:] + south[deep:] + far_north[rows:]
    ring = join(two[:deep], south[:deep], far_north[:rows], far_south, north[:deep])
    ring = ring.reshape(Y * XH, rows, block)
    mine = []
    for by in ORDER:
        other_place = (z + by + z) % COL
        at = (other_place + Y - y) % Y * XH + (other_place // Y + xh) % XH
        mine.append(lax.dynamic_index_in_dim(ring, at, 0, keepdims=False))
    mine = join(*mine)
    others, diag_other = tie(to_core(mine), to_core(diag))
    diag = (diag + diag_other)[:1]
    xr_own, xr_other = join(*x_ring), join(x_first, x_last)
    symmetric += contract(join(up3, down3, far_up, far_down), x_cols[cut:], 0, 0)
    symmetric += contract(jnp.where(core == s, xr_own, xr_other), mine, 0, 0)
    symmetric += contract(jnp.where(core == s, xr_other, xr_own), others, 0, 0)
    inverse_diag = jnp.where(on_diagonal, 1.0 / jnp.where(on_diagonal, prec_half, 1.0), 0.0)
    gradient = symmetric / (2.0 * sample_count) - inverse_diag
    stepped = prec_half - step_size * gradient
    orders = ngram_order.astype(jnp.float32)
    order_rows = lax.dynamic_slice_in_dim(orders, row_index * block, block, 0)
    order_cols = lax.dynamic_slice_in_dim(orders, own_block * block, block, 0)
    threshold = step_size * penalty * 0.5 * (order_rows[:, None] + order_cols[None, :])
    shrunk = jnp.sign(stepped) * jnp.maximum(jnp.abs(stepped) - threshold, 0.0)
    updated = jnp.where(on_diagonal, stepped, shrunk)

    partial = contract(new_rows, updated, 1, 0)
    out_rows = partial.shape[0] // (XH * Y * CORE)
    partial = partial.reshape(XH * Y, CORE, out_rows, block)
    kept = lax.dynamic_index_in_dim(partial, core, 1, keepdims=False)
    kept = kept + to_core(lax.dynamic_index_in_dim(partial, 1 - core, 1, keepdims=False))

    def part(dx, dy):
        target = (xh + dx) % XH * Y + (y + dy) % Y
        return lax.dynamic_index_in_dim(kept, target, 0, keepdims=False)

    total = part(0, 0)
    for dx in range(XH):
        for dy in range(Y):
            if dx or dy:
                total = total + to_plane(part(dx, dy), dx, dy)
    return (updated, total / diag)


def solution(mesh):
    placed = (P("row", "col"), P("rep", "col"), P(None, "row"), P())
    return jax.shard_map(
        per_device,
        mesh=mesh,
        in_specs=placed,
        out_specs=(P("row", ("col", "rep")), P("row", ("col", "rep"))),
        check_vma=False,
    )
```
